32 devices in a mesh: group: 2 (over y), role: 2 (over core), dev: 8 (over z, x).
Axes of the slice: x: 2, y: 2, z: 4, core: 2. Of those that a mesh axis runs over, the one named last changes fastest.
Arguments:
- hidden: bfloat16 [64, 7168], P(('group', 'role', 'dev')), parts along dimension 0, may hold values from -6 to 6
- norm_gain: bfloat16 [7168], replicated, may hold values from 0.099609375 to 1.8984375
- routes: int32 [64, 8], P(('group', 'role', 'dev')), parts along dimension 0, may hold values from 0 to 15, all different within a row; in each aligned block of 2 rows (0 to 1, 2 to 3, ...) at most 2 rows name the same one
- gate_weights: float32 [64, 8], P(('group', 'role', 'dev')), parts along dimension 0, may hold values from 0.1 to 0.5
- w_gate: bfloat16 [7168, 32768], P(None, ('role', 'dev')), may hold values from -0.0625 to 0.0625
- w_up: bfloat16 [7168, 32768], P(None, ('role', 'dev')), may hold values from -0.0625 to 0.0625
- w_down: bfloat16 [32768, 7168], P(('role', 'dev')), may hold values from -0.125 to 0.125
- queries: bfloat16 [64, 64, 576], P(('group', 'role', 'dev')), parts along dimension 0, may hold values from -48 to 48
- local_cache: bfloat16 [64, 64, 576], P(('group', 'role', 'dev')), parts along dimension 0, may hold values from -6 to 6
- cache_lengths: int32 [64], P(('group', 'role', 'dev')), parts along dimension 0, may hold values from 2 to 64
- swap_pool: bfloat16 [512, 16, 576], P(('group', 'role', 'dev')), parts along dimension 0, may hold values from -6 to 6
- page_ids: int32 [32, 16], P(('group', 'role', 'dev')), parts along dimension 0, may hold values from 0 to 15
- page_owner: int32 [32, 16], P(('group', 'role', 'dev')), parts along dimension 0, may hold values from 0 to 1
Outputs:
- attn_out: bfloat16 [64, 64, 512], P(('group', 'role', 'dev')), parts along dimension 0
- moe_out: bfloat16 [64, 7168], P(('group', 'role', 'dev')), parts along dimension 0
The draws below stay inside these ranges and needn't reach their ends.
There are 2 independent parts, one for each index of `group`. The reference program is written for one: setup_inputs(seed, part) draws one part's arguments, and reference() takes and returns one part's arrays. A program takes and returns all parts, laid end to end along the dimension named above; an argument that names none is the same for every part. Nothing has to cross between parts.
Inputs may be any that keep to these rules, and one draw needn't show every extreme that they name: `routes`: each row names 8 different experts; in the rows of one device no expert is named more than 2 times. `page_ids`: every device receives exactly one page from every holder.
All inputs are finite; a program needn't handle non-finite values.
Results may differ from the reference program's by a relative error of at most 0.0046.
Values may be sent and summed in bfloat16 or wider, within the bound.
A program may use at most 128 MiB of HBM per device.

```python
import math
import jax
import jax.numpy as jnp
import numpy as np
from jax import lax

D = 7168
LAT = 512
ROPE = 64
EWIN = 2048
TOP = 8
HEADS = 64
EXPERTS = 16
PAGE = 16
REQ_DEV = 2
LOCAL_LEN = 64
POOL = 16
CAP = 2
ROWS = 32
POOL_ALL = 256
N_ROLE = 2
N_DEV = 8


def attention_draws(key):
    channels = LAT + ROPE
    subkeys = jax.random.split(jax.random.fold_in(key, 9151), 2)
    latents = jnp.clip(jax.random.normal(subkeys[0], (ROWS, LOCAL_LEN, channels), jnp.float32), -6.0, 6.0)
    queries = jnp.clip(jax.random.normal(subkeys[1], (ROWS, HEADS, channels), jnp.float32), -6.0, 6.0)
    return (queries, latents)


def draw_queries(key, part):
    return attention_draws(key)[0].astype(jnp.bfloat16)


def draw_local_cache(key, part):
    return attention_draws(key)[1].astype(jnp.bfloat16)


def plant(array, rng, low, largest):
    spot = [jax.random.randint(jax.random.fold_in(rng, axis), (), 0, length) for axis, length in enumerate(array.shape)]
    main_axis = array.shape.index(max(array.shape))
    neighbour = spot[:main_axis] + [(spot[main_axis] + 1) % array.shape[main_axis]] + spot[main_axis + 1:]
    return array.at[tuple(spot)].set(low).at[tuple(neighbour)].set(largest)


def levels(own_key, extent, pieces, smallest, top_value):
    gain, own = 1.0, jax.random.fold_in(own_key, 6)
    for dim, blocks in pieces:
        heights = jnp.exp(jax.random.uniform(jax.random.fold_in(own, dim), (blocks,), jnp.float32, smallest / len(pieces), top_value / len(pieces)))
        gain = gain * jnp.repeat(heights, extent[dim] // blocks).reshape([-1 if axis == dim else 1 for axis in range(len(extent))])
    return gain


def cumulative_ranks(number_of, slope):
    portions = [(1 << 20) // math.isqrt(standing ** slope) + 1 for standing in range(1, number_of + 1)]
    width = 1 + sum(portions) // (1 << 30)
    return np.cumsum(np.array([max(1, weight // width) for weight in portions]))


def skewed_ids(rng, dims, amount, slope):
    table = cumulative_ranks(amount, slope)
    ticket = jax.random.randint(jax.random.fold_in(rng, 1), dims, 0, int(table[amount - 1]))
    grade = jnp.searchsorted(jnp.asarray(table, jnp.int32), ticket, side="right")
    return jax.random.permutation(jax.random.fold_in(rng, 2), amount)[grade].astype(jnp.int32)


def routed_block(own_key, own, number, rows, number_of, top, most, slope):
    ranking = jax.random.permutation(own_key, number_of)
    heavy_load, ordinary = portions_of(number_of, rows * top, most, slope, True), portions_of(number_of, rows * top, most, slope, False)
    places = jnp.arange(number_of)

    def named(sizes, offset_by):
        used = int((sizes > 0).sum())
        fixed = max(1, used // 4)
        moved = fixed + (places - fixed + offset_by * (used - fixed)) % max(1, number_of - fixed)
        return jnp.zeros((number_of,), jnp.int32).at[ranking[jnp.where(places < fixed, places, moved)]].set(jnp.asarray(sizes, jnp.int32))

    sizes = jnp.where(number % 4 == 0, named(heavy_load, number // 4), named(ordinary, number - number // 4 - 1))
    mixed = jax.random.permutation(jax.random.fold_in(own, 3), number_of)
    giver, sink = mixed[0:number_of // 2 * 2:2], mixed[1:number_of // 2 * 2:2]
    margin = jnp.minimum(sizes[giver] - 1, most - sizes[sink]) // 2
    margin = jnp.where((giver == ranking[0]) | (sink == ranking[0]) | (sizes[sink] == 0), 0, jnp.maximum(margin, 0))
    moved = jax.random.randint(jax.random.fold_in(own, 4), (number_of // 2,), 0, 1 << 20) % (margin + 1)
    sizes = sizes.at[giver].add(-moved).at[sink].add(moved)
    items = jnp.searchsorted(jnp.cumsum(sizes), jnp.arange(rows * top), side="right").astype(jnp.int32)
    table = items.reshape(top, rows).T
    table = table[jax.random.permutation(jax.random.fold_in(own, 1), rows)]
    offset_by = jax.random.randint(jax.random.fold_in(own, 2), (rows, 1), 0, top)
    return jnp.take_along_axis(table, (jnp.arange(top)[None, :] + offset_by) % top, axis=1)


def portions_of(amount, total, most, lean, full):
    loads = [(1 << 20) // math.isqrt(standing ** lean) + 1 for standing in range(1, amount + 1)]
    largest = most if full else min(most, max(-(-total // amount), total * loads[0] // sum(loads)))
    least = 1 if total - largest >= amount - 1 else 0
    given, surplus = [largest] + [least] * (amount - 1), total - largest - least * (amount - 1)
    while surplus > 0:
        movable = [i for i in range(1, amount) if given[i] < largest] or [i for i in range(1, amount) if given[i] < most]
        pool, budget = sum([loads[i] for i in movable]), surplus
        for i in movable:
            more = min(most - given[i], max(1, budget * loads[i] // pool), surplus)
            given[i] = given[i] + more
            surplus = surplus - more
    return np.array(given)


def bell_draw(stream_key, shape, scale, limit, shards=(), kind=jnp.bfloat16):
    values = scale * jax.random.normal(stream_key, shape, jnp.float32)
    if shards:
        values = values * levels(stream_key, shape, shards, -0.22, 0.18)
    return jnp.clip(values, -limit, limit).astype(kind)


def setup_inputs(seed: int = 0, part: int = 0) -> dict:
    streams_of = jax.random.split(jax.random.key(seed), 14)
    part_keys = jax.random.split(jax.random.fold_in(streams_of[13], part), 14)
    hidden = bell_draw(part_keys[0], (ROWS, D), 1.0, 6.0, ((0, 16),))
    norm_gain = jnp.clip(1.0 + 0.18 * jax.random.normal(streams_of[1], (D,), jnp.float32), 0.099609375, 1.8984375).astype(jnp.bfloat16)
    routes_keys = jax.random.split(jax.random.fold_in(part_keys[2], 1), ROWS // REQ_DEV)
    routes_turns = jax.random.permutation(jax.random.fold_in(part_keys[2], 3), ROWS // REQ_DEV)
    routes = jax.vmap(lambda own, number: routed_block(jax.random.fold_in(part_keys[2], 2), own, number, REQ_DEV, EXPERTS, TOP, CAP, 2))(routes_keys, routes_turns).reshape((ROWS, TOP))
    gate_weights = jnp.clip(0.1 + 0.4 * jax.random.uniform(part_keys[3], (ROWS, TOP), jnp.float32) ** levels(part_keys[3], (ROWS, TOP), ((0, 16),), -0.2, 0.2), 0.1, 0.5)
    w_gate = bell_draw(streams_of[4], (D, EXPERTS * EWIN), D ** -0.5, 0.0625, ((1, 16),))
    w_up = bell_draw(streams_of[5], (D, EXPERTS * EWIN), D ** -0.5, 0.0625, ((1, 16),))
    w_down = bell_draw(streams_of[6], (EXPERTS * EWIN, D), EWIN ** -0.5, 0.125, ((0, 16),))
    queries = draw_queries(jax.random.fold_in(jax.random.fold_in(streams_of[13], part), 71), part)
    local_cache = draw_local_cache(jax.random.fold_in(jax.random.fold_in(streams_of[13], part), 71), part)
    cache_lengths = plant(jax.random.randint(part_keys[9], (ROWS,), 2, LOCAL_LEN + 1), jax.random.fold_in(part_keys[9], 1), 2, LOCAL_LEN).astype(jnp.int32)
    swap_pool = bell_draw(part_keys[10], (POOL_ALL, PAGE, LAT + ROPE), 1.0, 6.0, ((0, 16),))
    page_ids = plant(jax.random.randint(part_keys[11], (N_ROLE * N_DEV, N_ROLE * N_DEV), 0, POOL), jax.random.fold_in(part_keys[11], 1), 0, POOL - 1).astype(jnp.int32)
    page_owner = plant(skewed_ids(part_keys[12], (N_ROLE * N_DEV, N_ROLE * N_DEV), REQ_DEV, 2), jax.random.fold_in(part_keys[12], 3), 0, REQ_DEV - 1).astype(jnp.int32)
    return dict(hidden=hidden, norm_gain=norm_gain, routes=routes, gate_weights=gate_weights, w_gate=w_gate, w_up=w_up, w_down=w_down, queries=queries, local_cache=local_cache, cache_lengths=cache_lengths, swap_pool=swap_pool, page_ids=page_ids, page_owner=page_owner)


score_scale = 192.0 ** (-0.5)
norm_eps = 1e-06

def device_attention(queries, local_cache, cache_lengths, fetched, owners):
    query_wide = queries.astype(jnp.float32)
    local_scores = jnp.einsum('rhc,rtc->rht', query_wide, local_cache.astype(jnp.float32)) * score_scale
    positions = jnp.arange(local_cache.shape[1], dtype=jnp.int32)
    local_valid = positions[None, None, :] < cache_lengths[:, None, None]
    local_scores = jnp.where(local_valid, local_scores, -jnp.inf)
    page_query = queries[owners]
    page_scores = jnp.einsum('phc,ptc->pht', page_query.astype(jnp.float32), fetched.astype(jnp.float32)) * score_scale
    request_ids = jnp.arange(queries.shape[0], dtype=jnp.int32)
    belongs = owners[None, :] == request_ids[:, None]
    page_peak = lax.optimization_barrier(jnp.max(page_scores, axis=2))
    owned_peak = lax.optimization_barrier(jnp.max(jnp.where(belongs[:, :, None], page_peak[None], -jnp.inf), axis=1))
    row_peak = jnp.maximum(lax.optimization_barrier(jnp.max(local_scores, axis=2)), owned_peak)
    local_exp = jnp.exp(local_scores - row_peak[:, :, None])
    page_exp = jnp.exp(page_scores - row_peak[owners][:, :, None])
    page_total = lax.optimization_barrier(jnp.sum(page_exp, axis=2))
    owned_total = lax.optimization_barrier(jnp.sum(jnp.where(belongs[:, :, None], page_total[None], 0.0), axis=1))
    normalizer = lax.optimization_barrier(jnp.sum(local_exp, axis=2)) + owned_total
    local_probs = (local_exp / normalizer[:, :, None]).astype(jnp.bfloat16)
    page_probs = (page_exp / normalizer[owners][:, :, None]).astype(jnp.bfloat16)
    local_part = jnp.einsum('rht,rtc->rhc', local_probs.astype(jnp.float32), local_cache[:, :, :LAT].astype(jnp.float32))
    page_part = jnp.einsum('pht,ptc->phc', page_probs.astype(jnp.float32), fetched[:, :, :LAT].astype(jnp.float32))
    owned_part = jnp.einsum('rp,phc->rhc', belongs.astype(jnp.float32), page_part, precision=lax.Precision.HIGHEST)
    return (local_part + owned_part).astype(jnp.bfloat16)

def reference(hidden, norm_gain, routes, gate_weights, w_gate, w_up, w_down, queries, local_cache, cache_lengths, swap_pool, page_ids, page_owner):
    devices = N_ROLE * N_DEV
    channels = LAT + ROPE
    pool_blocks = swap_pool.reshape(devices, POOL, PAGE, channels)
    query_blocks = queries.reshape(devices, REQ_DEV, HEADS, channels)
    cache_blocks = local_cache.reshape(devices, REQ_DEV, LOCAL_LEN, channels)
    length_blocks = cache_lengths.reshape(devices, REQ_DEV)
    sources = jnp.arange(devices, dtype=jnp.int32)

    def one_device(packed):
        query_block, cache_block, length_block, id_row, owner_row = packed
        fetched = pool_blocks[sources, id_row]
        return device_attention(query_block, cache_block, length_block, fetched, owner_row)
    attention = lax.map(one_device, (query_blocks, cache_blocks, length_blocks, page_ids, page_owner))
    attn_out = attention.reshape(ROWS, HEADS, LAT)
    hidden_wide = hidden.astype(jnp.float32)
    inv_rms = lax.rsqrt(lax.optimization_barrier(jnp.mean(hidden_wide * hidden_wide, axis=1, keepdims=True)) + norm_eps)
    normed = (hidden_wide * inv_rms * norm_gain.astype(jnp.float32)[None, :]).astype(jnp.bfloat16)
    expert_ids = jnp.arange(EXPERTS, dtype=jnp.int32)

    def add_expert(running, expert):
        start = (expert * EWIN).astype(jnp.int32)
        gate_cols = lax.dynamic_slice_in_dim(w_gate, start, EWIN, 1)
        up_cols = lax.dynamic_slice_in_dim(w_up, start, EWIN, 1)
        down_rows = lax.dynamic_slice_in_dim(w_down, start, EWIN, 0)
        gate_proj = jnp.dot(normed, gate_cols, preferred_element_type=jnp.float32)
        up_proj = jnp.dot(normed, up_cols, preferred_element_type=jnp.float32)
        act_units = (jax.nn.silu(gate_proj) * up_proj).astype(jnp.bfloat16)
        output = jnp.dot(act_units, down_rows, preferred_element_type=jnp.float32)
        weight = lax.optimization_barrier(jnp.sum(jnp.where(routes == expert, gate_weights, 0.0), axis=1))
        return (running + weight[:, None] * output, None)
    running, _ = lax.scan(add_expert, jnp.zeros((ROWS, D), jnp.float32), expert_ids)
    moe_out = (hidden_wide + running).astype(jnp.bfloat16)
    return (attn_out, moe_out)
```

```python
import functools

import jax
import jax.numpy as jnp
from jax import lax
from jax.experimental import pallas as pl
from jax.experimental.pallas import tpu as pltpu
from jax.sharding import PartitionSpec as P

ROPE = 64
EXPERTS = 16
TILE = 16
LANES = 128
AHEAD = 4


score_scale = 192.0 ** (-0.5)
norm_eps = 1e-06


def iota(shape, axis):
    return lax.broadcasted_iota(jnp.int32, shape, axis)


def div(value, power):
    return value >> (power.bit_length() - 1)


def mod(value, power):
    return value & (power - 1)


def layer_kernel(
    sizes,
    hidden_ref,
    gain_ref,
    ids_ref,
    routes_ref,
    mix_ref,
    lengths_ref,
    owner_ref,
    queries_hbm,
    cache_hbm,
    pool_hbm,
    gate_hbm,
    up_hbm,
    down_hbm,
    attn_ref,
    moe_ref,
    gate_buf,
    up_buf,
    down_buf,
    queries_buf,
    cache_buf,
    pool_buf,
    packed,
    row_send,
    row_recv,
    row_parts,
    gate_acc,
    up_acc,
    units,
    ids_send,
    ids_recv,
    page_send,
    page_recv,
    out_send,
    out_recv,
    out_wide,
    gate_sem,
    up_sem,
    down_sem,
    small_sem,
    ids_sems,
    row_sems,
    page_sems,
    out_send_sem,
    out_recv_sem,
):
    roles, devs = sizes
    n = roles * devs
    rows, width = hidden_ref.shape
    subs = TILE // rows
    part = width // subs
    chunk = subs * LANES
    chunks = width // chunk
    block = min(n, 16)
    block_rows = block * rows
    me = lax.axis_index("role") * devs + lax.axis_index("dev")

    def target(step):
        peer = lax.rem(me + step, n)
        return peer, {"role": peer // devs, "dev": lax.rem(peer, devs)}

    def gate_copy(s):
        return pltpu.make_async_copy(
            gate_hbm.at[pl.ds(s * part, part), :],
            gate_buf.at[lax.rem(s, AHEAD)],
            gate_sem.at[lax.rem(s, AHEAD)],
        )

    def up_copy(s):
        return pltpu.make_async_copy(
            up_hbm.at[pl.ds(s * part, part), :],
            up_buf.at[lax.rem(s, AHEAD)],
            up_sem.at[lax.rem(s, AHEAD)],
        )

    def down_copy(c):
        return pltpu.make_async_copy(
            down_hbm.at[:, pl.ds(pl.multiple_of(c * chunk, chunk), chunk)],
            down_buf.at[c],
            down_sem.at[c],
        )

    small = [
        pltpu.make_async_copy(source, dest, small_sem.at[i])
        for i, (source, dest) in enumerate(
            ((pool_hbm, pool_buf), (queries_hbm, queries_buf), (cache_hbm, cache_buf))
        )
    ]
    barrier = pltpu.get_barrier_semaphore()

    def greet(step, carry):
        _, device = target(step)
        pl.semaphore_signal(barrier, inc=1, device_id=device, device_id_type=pl.DeviceIdType.MESH)
        return carry

    lax.fori_loop(1, n, greet, 0)
    for copy in small:
        copy.start()

    def first_weights(s, carry):
        gate_copy(s).start()
        up_copy(s).start()
        return carry

    lax.fori_loop(0, AHEAD, first_weights, 0)
    early = min(2, chunks)
    for c in range(early):
        down_copy(c).start()

    ids_send[...] = jnp.zeros_like(ids_send)
    ids_send[:, 0:n] = jnp.broadcast_to(ids_ref[...], (8, n))
    hidden_wide = hidden_ref[...].astype(jnp.float32)
    inv_rms = lax.rsqrt(jnp.mean(hidden_wide * hidden_wide, axis=1, keepdims=True) + norm_eps)
    normed = hidden_wide * inv_rms * gain_ref[...].astype(jnp.float32)
    for r in range(rows):
        for s in range(subs):
            packed[r * subs + s : r * subs + s + 1, :] = normed[r : r + 1, s * part : (s + 1) * part]
    row_send[...] = packed[...].astype(jnp.bfloat16)
    own = pl.ds(pl.multiple_of(me * TILE, TILE), TILE)
    row_recv[own, :] = row_send[...]
    ids_recv[me] = ids_send[...]
    pl.semaphore_wait(barrier, n - 1)

    def send_all(source_of, dest, send_sem, recv_sem):
        def send(step, carry):
            peer, device = target(step)
            pltpu.make_async_remote_copy(
                src_ref=source_of(peer),
                dst_ref=dest,
                send_sem=send_sem,
                recv_sem=recv_sem,
                device_id=device,
                device_id_type=pl.DeviceIdType.MESH,
            ).start()
            return carry

        lax.fori_loop(1, n, send, 0)

    def wait_all(ref, sem):
        pltpu.make_async_copy(ref, ref, sem).wait()

    others = pl.ds(0, (n - 1) * TILE)
    send_all(lambda peer: ids_send, ids_recv.at[me], ids_sems.at[0], ids_sems.at[1])
    send_all(lambda peer: row_send, row_recv.at[own, :], row_sems.at[0], row_sems.at[1])

    def peer_rows(peer):
        return pl.ds(pl.multiple_of(peer * TILE, TILE), TILE)

    small[0].wait()
    wait_all(ids_recv.at[pl.ds(0, n - 1)], ids_sems.at[1])
    ids_all = ids_recv[...]
    wanted = jnp.sum(jnp.where(iota(ids_all.shape, 2) == me, ids_all, 0), axis=2, keepdims=True)
    wanted = jnp.concatenate([wanted, wanted], axis=1).reshape(n * TILE, 1)
    pool_rows = pool_buf[...].reshape(-1, pool_buf.shape[2])
    pick = (n * TILE, pool_rows.shape[0])
    chosen = (wanted == div(iota(pick, 1), TILE)) & (
        mod(iota(pick, 0), TILE) == mod(iota(pick, 1), TILE)
    )
    page_send[...] = jnp.dot(
        jnp.where(chosen, 1.0, 0.0).astype(jnp.bfloat16),
        pool_rows,
        preferred_element_type=jnp.float32,
    ).astype(jnp.bfloat16)
    send_all(
        lambda peer: page_send.at[peer_rows(peer), :],
        page_recv.at[own, :],
        page_sems.at[0],
        page_sems.at[1],
    )
    page_recv[own, :] = page_send[own, :]

    square = (block * TILE, block * TILE)

    def place(index):
        return mod(index, block_rows) * subs + div(index, block_rows)

    to_parts = jnp.where(place(iota(square, 0)) == iota(square, 1), 1.0, 0.0).astype(jnp.bfloat16)
    to_packed = jnp.where(iota(square, 0) == place(iota(square, 1)), 1.0, 0.0).astype(jnp.bfloat16)

    wait_all(row_recv.at[others, :], row_sems.at[1])
    for b in range(n // block):
        moved = jnp.dot(
            to_parts,
            row_recv[b * block * TILE : (b + 1) * block * TILE, :],
            preferred_element_type=jnp.float32,
        ).astype(jnp.bfloat16)
        for s in range(subs):
            row_parts[s, b * block_rows : (b + 1) * block_rows, :] = moved[
                s * block_rows : (s + 1) * block_rows, :
            ]

    gate_acc[...] = jnp.zeros_like(gate_acc)
    up_acc[...] = jnp.zeros_like(up_acc)

    def project(s, carry):
        slot = lax.rem(s, AHEAD)
        x = row_parts[s]
        gate_copy(s).wait()
        gate_acc[...] += jnp.dot(x, gate_buf[slot], preferred_element_type=jnp.float32)
        up_copy(s).wait()
        up_acc[...] += jnp.dot(x, up_buf[slot], preferred_element_type=jnp.float32)

        @pl.when(s + AHEAD < subs)
        def _():
            gate_copy(s + AHEAD).start()
            up_copy(s + AHEAD).start()

        @pl.when(s == max(subs - AHEAD - 1, 0))
        def _():
            for c in range(early, chunks):
                down_copy(c).start()

        return carry

    lax.fori_loop(0, subs, project, 0)
    gate = gate_acc[...]
    units[...] = (gate / (1.0 + jnp.exp(-gate)) * up_acc[...]).astype(jnp.bfloat16)

    def expand(c, carry):
        down_copy(c).wait()
        partial = jnp.dot(units[...], down_buf[c], preferred_element_type=jnp.float32).astype(
            jnp.bfloat16
        )
        for b in range(n // block):
            stacked = jnp.concatenate(
                [
                    partial[b * block_rows : (b + 1) * block_rows, q * LANES : (q + 1) * LANES]
                    for q in range(subs)
                ],
                axis=0,
            )
            out_send[c, b * block * TILE : (b + 1) * block * TILE, :] = jnp.dot(
                to_packed, stacked, preferred_element_type=jnp.float32
            ).astype(jnp.bfloat16)
        send_all(
            lambda peer: out_send.at[c, peer_rows(peer), :],
            out_recv.at[c, own, :],
            out_send_sem.at[c],
            out_recv_sem.at[c],
        )
        out_recv[c, own, :] = out_send[c, own, :]
        return carry

    lax.fori_loop(0, chunks, expand, 0)

    small[1].wait()
    small[2].wait()
    wait_all(page_recv.at[others, :], page_sems.at[1])
    pages = page_recv[...]
    latent = pages.shape[1] - ROPE
    transposed = (((1,), (1,)), ((), ()))
    holder = div(iota((1, n * TILE), 1), TILE)
    owner = jnp.zeros((1, n * TILE), jnp.int32)
    for p in range(n):
        owner = jnp.where(holder == p, owner_ref[0, p], owner)
    for r in range(rows):
        query = queries_buf[r]
        cache = cache_buf[r]
        page_scores = (
            lax.dot_general(query, pages, transposed, preferred_element_type=jnp.float32)
            * score_scale
        )
        page_scores = jnp.where(owner == r, page_scores, -jnp.inf)
        local_scores = (
            lax.dot_general(query, cache, transposed, preferred_element_type=jnp.float32)
            * score_scale
        )
        position = iota((1, cache.shape[0]), 1)
        local_scores = jnp.where(position < lengths_ref[r], local_scores, -jnp.inf)
        peak = jnp.maximum(
            jnp.max(page_scores, axis=1, keepdims=True), jnp.max(local_scores, axis=1, keepdims=True)
        )
        page_exp = jnp.exp(page_scores - peak)
        local_exp = jnp.exp(local_scores - peak)
        total = jnp.sum(page_exp, axis=1, keepdims=True) + jnp.sum(local_exp, axis=1, keepdims=True)
        attn_ref[r] = (
            jnp.dot(
                (page_exp / total).astype(jnp.bfloat16),
                pages[:, :latent],
                preferred_element_type=jnp.float32,
            )
            + jnp.dot(
                (local_exp / total).astype(jnp.bfloat16),
                cache[:, :latent],
                preferred_element_type=jnp.float32,
            )
        ).astype(jnp.bfloat16)

    table = (TILE, n * TILE)
    row_of = div(iota(table, 0), subs)
    expert_of = div(div(iota(table, 1), TILE), n // EXPERTS)
    weight = jnp.zeros(table, jnp.float32)
    for k in range(routes_ref.shape[1]):
        route = jnp.zeros(table, jnp.int32)
        mix = jnp.zeros(table, jnp.float32)
        for r in range(rows):
            route = jnp.where(row_of == r, routes_ref[r, k], route)
            mix = jnp.where(row_of == r, mix_ref[r, k], mix)
        weight += jnp.where(route == expert_of, mix, 0.0)
    weight = jnp.where(iota(table, 0) == mod(iota(table, 1), TILE), weight, 0.0)
    high = weight.astype(jnp.bfloat16)
    low = (weight - high.astype(jnp.float32)).astype(jnp.bfloat16)
    for c in range(chunks):
        wait_all(out_recv.at[c, others, :], out_recv_sem.at[c])
        got = out_recv[c]
        mixed = jnp.dot(high, got, preferred_element_type=jnp.float32) + jnp.dot(
            low, got, preferred_element_type=jnp.float32
        )
        for r in range(rows):
            for q in range(subs):
                out_wide[r : r + 1, c * chunk + q * LANES : c * chunk + (q + 1) * LANES] = mixed[
                    r * subs + q : r * subs + q + 1, :
                ]
    moe_ref[...] = (hidden_ref[...].astype(jnp.float32) + out_wide[...]).astype(jnp.bfloat16)

    wait_all(ids_recv.at[pl.ds(0, n - 1)], ids_sems.at[0])
    wait_all(row_recv.at[others, :], row_sems.at[0])
    wait_all(page_send.at[others, :], page_sems.at[0])
    for c in range(chunks):
        wait_all(out_send.at[c, others, :], out_send_sem.at[c])


def per_device(
    sizes,
    hidden,
    norm_gain,
    routes,
    gate_weights,
    w_gate,
    w_up,
    w_down,
    queries,
    local_cache,
    cache_lengths,
    swap_pool,
    page_ids,
    page_owner,
):
    n = sizes[0] * sizes[1]
    rows, width = hidden.shape
    total = rows * n
    hidden_units = w_gate.shape[1]
    channels = queries.shape[2]
    subs = TILE // rows
    part = width // subs
    chunk = subs * LANES
    chunks = width // chunk
    id_lanes = -(-n // LANES) * LANES
    vmem = pl.BlockSpec(memory_space=pltpu.VMEM)
    smem = pl.BlockSpec(memory_space=pltpu.SMEM)
    hbm = pl.BlockSpec(memory_space=pl.ANY)
    bf16, f32 = jnp.bfloat16, jnp.float32
    dma = pltpu.SemaphoreType.DMA
    return pl.pallas_call(
        functools.partial(layer_kernel, sizes),
        out_shape=(
            jax.ShapeDtypeStruct(queries.shape[:2] + (channels - ROPE,), bf16),
            jax.ShapeDtypeStruct(hidden.shape, bf16),
        ),
        in_specs=[vmem] * 3 + [smem] * 4 + [hbm] * 6,
        out_specs=(vmem, vmem),
        scratch_shapes=[
            pltpu.VMEM((AHEAD, part, hidden_units), bf16),
            pltpu.VMEM((AHEAD, part, hidden_units), bf16),
            pltpu.VMEM((chunks, hidden_units, chunk), bf16),
            pltpu.VMEM(queries.shape, bf16),
            pltpu.VMEM(local_cache.shape, bf16),
            pltpu.VMEM(swap_pool.shape, bf16),
            pltpu.VMEM((TILE, part), f32),
            pltpu.VMEM((TILE, part), bf16),
            pltpu.VMEM((n * TILE, part), bf16),
            pltpu.VMEM((subs, total, part), bf16),
            pltpu.VMEM((total, hidden_units), f32),
            pltpu.VMEM((total, hidden_units), f32),
            pltpu.VMEM((total, hidden_units), bf16),
            pltpu.VMEM((8, id_lanes), jnp.int32),
            pltpu.VMEM((n, 8, id_lanes), jnp.int32),
            pltpu.VMEM((n * TILE, channels), bf16),
            pltpu.VMEM((n * TILE, channels), bf16),
            pltpu.VMEM((chunks, n * TILE, LANES), bf16),
            pltpu.VMEM((chunks, n * TILE, LANES), bf16),
            pltpu.VMEM((rows, width), f32),
            dma((AHEAD,)),
            dma((AHEAD,)),
            dma((chunks,)),
            dma((3,)),
            dma((2,)),
            dma((2,)),
            dma((2,)),
            dma((chunks,)),
            dma((chunks,)),
        ],
        compiler_params=pltpu.CompilerParams(
            collective_id=0, has_side_effects=True, vmem_limit_bytes=63 * 1024 * 1024
        ),
    )(
        hidden,
        norm_gain.reshape(1, -1),
        page_ids,
        routes,
        gate_weights,
        cache_lengths,
        page_owner,
        queries,
        local_cache,
        swap_pool,
        w_gate,
        w_up,
        w_down,
    )


def solution(mesh):
    in_specs = (
        P(("group", "role", "dev"), None),
        P(),
        P(("group", "role", "dev"), None),
        P(("group", "role", "dev"), None),
        P(None, ("role", "dev")),
        P(None, ("role", "dev")),
        P(("role", "dev"), None),
        P(("group", "role", "dev"), None, None),
        P(("group", "role", "dev"), None, None),
        P(("group", "role", "dev")),
        P(("group", "role", "dev"), None, None),
        P(("group", "role", "dev"), None),
        P(("group", "role", "dev"), None),
    )
    out_specs = (P(("group", "role", "dev"), None, None), P(("group", "role", "dev"), None))
    sizes = (mesh.shape["role"], mesh.shape["dev"])
    return jax.shard_map(
        functools.partial(per_device, sizes),
        mesh=mesh,
        in_specs=in_specs,
        out_specs=out_specs,
        check_vma=False,
    )
```

```python
import functools

import jax
import jax.numpy as jnp
from jax import lax
from jax.experimental import pallas as pl
from jax.experimental.pallas import tpu as pltpu
from jax.sharding import PartitionSpec as P

ROPE = 64
EXPERTS = 16
TILE = 16
LANES = 128
AHEAD = 4


score_scale = 192.0 ** (-0.5)
norm_eps = 1e-06


def iota(shape, axis):
    return lax.broadcasted_iota(jnp.int32, shape, axis)


def div(value, power):
    return value >> (power.bit_length() - 1)


def mod(value, power):
    return value & (power - 1)


def layer_kernel(
    sizes,
    hidden_ref,
    gain_ref,
    ids_ref,
    routes_ref,
    mix_ref,
    lengths_ref,
    owner_ref,
    queries_hbm,
    cache_hbm,
    pool_hbm,
    gate_hbm,
    up_hbm,
    down_hbm,
    attn_ref,
    moe_ref,
    gate_buf,
    up_buf,
    down_buf,
    queries_buf,
    cache_buf,
    pool_buf,
    packed,
    row_send,
    row_recv,
    row_parts,
    gate_acc,
    up_acc,
    units,
    ids_send,
    ids_recv,
    page_send,
    page_recv,
    out_send,
    out_recv,
    out_wide,
    gate_sem,
    up_sem,
    down_sem,
    small_sem,
    ids_sems,
    row_sems,
    page_sems,
    out_send_sem,
    out_recv_sem,
):
    roles, devs = sizes
    n = roles * devs
    rows, width = hidden_ref.shape
    subs = TILE // rows
    part = width // subs
    chunk = subs * LANES
    chunks = width // chunk
    block = min(n, 16)
    block_rows = block * rows
    my_role, my_dev = lax.axis_index("role"), lax.axis_index("dev")
    me = my_role * devs + my_dev

    def target(step):
        peer = lax.rem(me + step, n)
        return peer, {"role": peer // devs, "dev": lax.rem(peer, devs)}

    def gate_copy(s):
        return pltpu.make_async_copy(
            gate_hbm.at[pl.ds(s * part, part), :],
            gate_buf.at[lax.rem(s, AHEAD)],
            gate_sem.at[lax.rem(s, AHEAD)],
        )

    def up_copy(s):
        return pltpu.make_async_copy(
            up_hbm.at[pl.ds(s * part, part), :],
            up_buf.at[lax.rem(s, AHEAD)],
            up_sem.at[lax.rem(s, AHEAD)],
        )

    def down_copy(c):
        return pltpu.make_async_copy(
            down_hbm.at[:, pl.ds(pl.multiple_of(c * chunk, chunk), chunk)],
            down_buf.at[c],
            down_sem.at[c],
        )

    small = [
        pltpu.make_async_copy(source, dest, small_sem.at[i])
        for i, (source, dest) in enumerate(
            ((pool_hbm, pool_buf), (queries_hbm, queries_buf), (cache_hbm, cache_buf))
        )
    ]
    barrier = pltpu.get_barrier_semaphore()

    def greet(step, carry):
        _, device = target(step)
        pl.semaphore_signal(barrier, inc=1, device_id=device, device_id_type=pl.DeviceIdType.MESH)
        return carry

    lax.fori_loop(1, n, greet, 0)
    for copy in small:
        copy.start()

    def first_weights(s, carry):
        gate_copy(s).start()
        up_copy(s).start()
        return carry

    lax.fori_loop(0, AHEAD, first_weights, 0)
    early = min(2, chunks)
    for c in range(early):
        down_copy(c).start()

    ids_send[...] = jnp.zeros_like(ids_send)
    ids_send[:, 0:n] = ids_ref[...]
    hidden_wide = hidden_ref[...].astype(jnp.float32)
    inv_rms = lax.rsqrt(jnp.mean(hidden_wide * hidden_wide, axis=1, keepdims=True) + norm_eps)
    normed = hidden_wide * inv_rms * gain_ref[...].astype(jnp.float32).reshape(1, width)
    for r in range(rows):
        for s in range(subs):
            packed[r * subs + s : r * subs + s + 1, :] = normed[r : r + 1, s * part : (s + 1) * part]
    row_send[...] = packed[...].astype(jnp.bfloat16)
    own = pl.ds(pl.multiple_of(me * TILE, TILE), TILE)
    row_recv[own, :] = row_send[...]
    ids_recv[me] = ids_send[...]
    pl.semaphore_wait(barrier, n - 1)

    def send_all(source_of, dest, send_sem, recv_sem):
        def send(step, carry):
            peer, device = target(step)
            pltpu.make_async_remote_copy(
                src_ref=source_of(peer),
                dst_ref=dest,
                send_sem=send_sem,
                recv_sem=recv_sem,
                device_id=device,
                device_id_type=pl.DeviceIdType.MESH,
            ).start()
            return carry

        lax.fori_loop(1, n, send, 0)

    def wait_all(ref, sem):
        pltpu.make_async_copy(ref, ref, sem).wait()

    others = pl.ds(0, (n - 1) * TILE)
    send_all(lambda peer: ids_send, ids_recv.at[me], ids_sems.at[0], ids_sems.at[1])

    def send_rows(step, carry):
        pltpu.make_async_remote_copy(
            src_ref=row_send,
            dst_ref=row_recv.at[own, :],
            send_sem=row_sems.at[0],
            recv_sem=row_sems.at[1],
            device_id={"dev": lax.rem(my_dev + step, devs)},
            device_id_type=pl.DeviceIdType.MESH,
        ).start()
        return carry

    lax.fori_loop(1, devs, send_rows, 0)
    crossed = row_recv.at[pl.ds(0, (devs - 1) * TILE), :]
    shared = row_recv.at[pl.ds(0, (roles - 1) * devs * TILE), :]

    def peer_rows(peer):
        return pl.ds(pl.multiple_of(peer * TILE, TILE), TILE)

    small[0].wait()
    wait_all(ids_recv.at[pl.ds(0, n - 1)], ids_sems.at[1])
    ids_all = ids_recv[...]
    wanted = jnp.sum(jnp.where(iota(ids_all.shape, 2) == me, ids_all, 0), axis=2, keepdims=True)
    wanted = jnp.broadcast_to(wanted, (n, TILE, 1)).reshape(n * TILE, 1)
    pool_rows = pool_buf[...].reshape(-1, pool_buf.shape[2])
    pick = (n * TILE, pool_rows.shape[0])
    chosen = (wanted == div(iota(pick, 1), TILE)) & (
        mod(iota(pick, 0), TILE) == mod(iota(pick, 1), TILE)
    )
    page_send[...] = jnp.dot(
        jnp.where(chosen, 1.0, 0.0).astype(jnp.bfloat16),
        pool_rows,
        preferred_element_type=jnp.float32,
    ).astype(jnp.bfloat16)
    square = (block * TILE, block * TILE)

    def place(index):
        return mod(index, block_rows) * subs + div(index, block_rows)

    to_parts = jnp.where(place(iota(square, 0)) == iota(square, 1), 1.0, 0.0).astype(jnp.bfloat16)
    to_packed = jnp.where(iota(square, 0) == place(iota(square, 1)), 1.0, 0.0).astype(jnp.bfloat16)

    wait_all(crossed, row_sems.at[1])
    mine = pl.ds(pl.multiple_of(my_role * devs * TILE, TILE), devs * TILE)
    for step in range(1, roles):
        pltpu.make_async_remote_copy(
            src_ref=row_recv.at[mine, :],
            dst_ref=row_recv.at[mine, :],
            send_sem=row_sems.at[2],
            recv_sem=row_sems.at[3],
            device_id={"role": lax.rem(my_role + step, roles)},
            device_id_type=pl.DeviceIdType.MESH,
        ).start()
    send_all(
        lambda peer: page_send.at[peer_rows(peer), :],
        page_recv.at[own, :],
        page_sems.at[0],
        page_sems.at[1],
    )
    page_recv[own, :] = page_send[own, :]
    wait_all(shared, row_sems.at[3])
    for b in range(n // block):
        moved = jnp.dot(
            to_parts,
            row_recv[b * block * TILE : (b + 1) * block * TILE, :],
            preferred_element_type=jnp.float32,
        ).astype(jnp.bfloat16)
        for s in range(subs):
            row_parts[s, b * block_rows : (b + 1) * block_rows, :] = moved[
                s * block_rows : (s + 1) * block_rows, :
            ]

    gate_acc[...] = jnp.zeros_like(gate_acc)
    up_acc[...] = jnp.zeros_like(up_acc)

    def project(s, carry):
        slot = lax.rem(s, AHEAD)
        x = row_parts[s]
        gate_copy(s).wait()
        gate_acc[...] += jnp.dot(x, gate_buf[slot], preferred_element_type=jnp.float32)
        up_copy(s).wait()
        up_acc[...] += jnp.dot(x, up_buf[slot], preferred_element_type=jnp.float32)

        @pl.when(s + AHEAD < subs)
        def _():
            gate_copy(s + AHEAD).start()
            up_copy(s + AHEAD).start()

        @pl.when(s == max(subs - AHEAD - 1, 0))
        def _():
            for c in range(early, chunks):
                down_copy(c).start()

        return carry

    lax.fori_loop(0, subs, project, 0)
    gate = gate_acc[...]
    units[...] = (gate / (1.0 + jnp.exp(-gate)) * up_acc[...]).astype(jnp.bfloat16)

    def expand(c, carry):
        down_copy(c).wait()
        partial = jnp.dot(units[...], down_buf[c], preferred_element_type=jnp.float32).astype(
            jnp.bfloat16
        )
        for b in range(n // block):
            stacked = jnp.concatenate(
                [
                    partial[b * block_rows : (b + 1) * block_rows, q * LANES : (q + 1) * LANES]
                    for q in range(subs)
                ],
                axis=0,
            )
            out_send[c, b * block * TILE : (b + 1) * block * TILE, :] = jnp.dot(
                to_packed, stacked, preferred_element_type=jnp.float32
            ).astype(jnp.bfloat16)
        send_all(
            lambda peer: out_send.at[c, peer_rows(peer), :],
            out_recv.at[c, own, :],
            out_send_sem.at[c],
            out_recv_sem.at[c],
        )
        out_recv[c, own, :] = out_send[c, own, :]
        return carry

    lax.fori_loop(0, chunks, expand, 0)

    small[1].wait()
    small[2].wait()
    wait_all(page_recv.at[others, :], page_sems.at[1])
    pages = page_recv[...]
    latent = pages.shape[1] - ROPE
    transposed = (((1,), (1,)), ((), ()))
    holder = div(iota((1, n * TILE), 1), TILE)
    owner = jnp.zeros((1, n * TILE), jnp.int32)
    for p in range(n):
        owner = jnp.where(holder == p, owner_ref[0, p], owner)
    for r in range(rows):
        query = queries_buf[r]
        cache = cache_buf[r]
        page_scores = (
            lax.dot_general(query, pages, transposed, preferred_element_type=jnp.float32)
            * score_scale
        )
        page_scores = jnp.where(owner == r, page_scores, -jnp.inf)
        local_scores = (
            lax.dot_general(query, cache, transposed, preferred_element_type=jnp.float32)
            * score_scale
        )
        position = iota((1, cache.shape[0]), 1)
        local_scores = jnp.where(position < lengths_ref[r], local_scores, -jnp.inf)
        peak = jnp.maximum(
            jnp.max(page_scores, axis=1, keepdims=True), jnp.max(local_scores, axis=1, keepdims=True)
        )
        page_exp = jnp.exp(page_scores - peak)
        local_exp = jnp.exp(local_scores - peak)
        total = jnp.sum(page_exp, axis=1, keepdims=True) + jnp.sum(local_exp, axis=1, keepdims=True)
        attn_ref[r] = (
            jnp.dot(
                (page_exp / total).astype(jnp.bfloat16),
                pages[:, :latent],
                preferred_element_type=jnp.float32,
            )
            + jnp.dot(
                (local_exp / total).astype(jnp.bfloat16),
                cache[:, :latent],
                preferred_element_type=jnp.float32,
            )
        ).astype(jnp.bfloat16)

    table = (TILE, n * TILE)
    row_of = div(iota(table, 0), subs)
    expert_of = div(div(iota(table, 1), TILE), n // EXPERTS)
    weight = jnp.zeros(table, jnp.float32)
    for k in range(routes_ref.shape[1]):
        route = jnp.zeros(table, jnp.int32)
        mix = jnp.zeros(table, jnp.float32)
        for r in range(rows):
            route = jnp.where(row_of == r, routes_ref[r, k], route)
            mix = jnp.where(row_of == r, mix_ref[r, k], mix)
        weight += jnp.where(route == expert_of, mix, 0.0)
    weight = jnp.where(iota(table, 0) == mod(iota(table, 1), TILE), weight, 0.0)
    high = weight.astype(jnp.bfloat16)
    low = (weight - high.astype(jnp.float32)).astype(jnp.bfloat16)
    for c in range(chunks):
        wait_all(out_recv.at[c, others, :], out_recv_sem.at[c])
        got = out_recv[c]
        mixed = jnp.dot(high, got, preferred_element_type=jnp.float32) + jnp.dot(
            low, got, preferred_element_type=jnp.float32
        )
        for r in range(rows):
            for q in range(subs):
                out_wide[r : r + 1, c * chunk + q * LANES : c * chunk + (q + 1) * LANES] = mixed[
                    r * subs + q : r * subs + q + 1, :
                ]
    moe_ref[...] = (hidden_ref[...].astype(jnp.float32) + out_wide[...]).astype(jnp.bfloat16)

    wait_all(ids_recv.at[pl.ds(0, n - 1)], ids_sems.at[0])
    wait_all(crossed, row_sems.at[0])
    wait_all(shared, row_sems.at[2])
    wait_all(page_send.at[others, :], page_sems.at[0])
    for c in range(chunks):
        wait_all(out_send.at[c, others, :], out_send_sem.at[c])


def hand_on(attn_ref, moe_ref, attn_out, moe_out):
    attn_out[...] = attn_ref[...]
    moe_out[...] = moe_ref[...]


def per_device(
    sizes,
    hidden,
    norm_gain,
    routes,
    gate_weights,
    w_gate,
    w_up,
    w_down,
    queries,
    local_cache,
    cache_lengths,
    swap_pool,
    page_ids,
    page_owner,
):
    n = sizes[0] * sizes[1]
    rows, width = hidden.shape
    total = rows * n
    hidden_units = w_gate.shape[1]
    channels = queries.shape[2]
    subs = TILE // rows
    part = width // subs
    chunk = subs * LANES
    chunks = width // chunk
    id_lanes = -(-n // LANES) * LANES
    vmem = pl.BlockSpec(memory_space=pltpu.VMEM)
    smem = pl.BlockSpec(memory_space=pltpu.SMEM)
    hbm = pl.BlockSpec(memory_space=pl.ANY)
    bf16, f32 = jnp.bfloat16, jnp.float32
    dma = pltpu.SemaphoreType.DMA
    attn_out, moe_out = pl.pallas_call(
        functools.partial(layer_kernel, sizes),
        out_shape=(
            jax.ShapeDtypeStruct(queries.shape[:2] + (channels - ROPE,), bf16),
            jax.ShapeDtypeStruct(hidden.shape, bf16),
        ),
        in_specs=[vmem] * 3 + [smem] * 4 + [hbm] * 6,
        out_specs=(vmem, vmem),
        scratch_shapes=[
            pltpu.VMEM((AHEAD, part, hidden_units), bf16),
            pltpu.VMEM((AHEAD, part, hidden_units), bf16),
            pltpu.VMEM((chunks, hidden_units, chunk), bf16),
            pltpu.VMEM(queries.shape, bf16),
            pltpu.VMEM(local_cache.shape, bf16),
            pltpu.VMEM(swap_pool.shape, bf16),
            pltpu.VMEM((TILE, part), f32),
            pltpu.VMEM((TILE, part), bf16),
            pltpu.VMEM((n * TILE, part), bf16),
            pltpu.VMEM((subs, total, part), bf16),
            pltpu.VMEM((total, hidden_units), f32),
            pltpu.VMEM((total, hidden_units), f32),
            pltpu.VMEM((total, hidden_units), bf16),
            pltpu.VMEM((1, id_lanes), jnp.int32),
            pltpu.VMEM((n, 1, id_lanes), jnp.int32),
            pltpu.VMEM((n * TILE, channels), bf16),
            pltpu.VMEM((n * TILE, channels), bf16),
            pltpu.VMEM((chunks, n * TILE, LANES), bf16),
            pltpu.VMEM((chunks, n * TILE, LANES), bf16),
            pltpu.VMEM((rows, width), f32),
            dma((AHEAD,)),
            dma((AHEAD,)),
            dma((chunks,)),
            dma((3,)),
            dma((2,)),
            dma((4,)),
            dma((2,)),
            dma((chunks,)),
            dma((chunks,)),
        ],
        compiler_params=pltpu.CompilerParams(
            collective_id=0, has_side_effects=True, vmem_limit_bytes=63 * 1024 * 1024
        ),
    )(
        hidden,
        norm_gain,
        page_ids,
        routes,
        gate_weights,
        cache_lengths,
        page_owner,
        queries,
        local_cache,
        swap_pool,
        w_gate,
        w_up,
        w_down,
    )
    return pl.pallas_call(
        hand_on,
        out_shape=(
            jax.ShapeDtypeStruct(attn_out.shape, bf16),
            jax.ShapeDtypeStruct(moe_out.shape, bf16),
        ),
        in_specs=[vmem, vmem],
        out_specs=(vmem, vmem),
    )(attn_out, moe_out)


def solution(mesh):
    in_specs = (
        P(("group", "role", "dev"), None),
        P(),
        P(("group", "role", "dev"), None),
        P(("group", "role", "dev"), None),
        P(None, ("role", "dev")),
        P(None, ("role", "dev")),
        P(("role", "dev"), None),
        P(("group", "role", "dev"), None, None),
        P(("group", "role", "dev"), None, None),
        P(("group", "role", "dev")),
        P(("group", "role", "dev"), None, None),
        P(("group", "role", "dev"), None),
        P(("group", "role", "dev"), None),
    )
    out_specs = (P(("group", "role", "dev"), None, None), P(("group", "role", "dev"), None))
    sizes = (mesh.shape["role"], mesh.shape["dev"])
    return jax.shard_map(
        functools.partial(per_device, sizes),
        mesh=mesh,
        in_specs=in_specs,
        out_specs=out_specs,
        check_vma=False,
    )
```
